512 devices in a mesh: loop: 32 (over y, z_hi, x), dp: 16 (over z_lo, core).
Axes of the slice: x: 4, y: 4, z: 16 (z_hi: 2, z_lo: 8; z = z_hi * 8 + z_lo), core: 2. Of those that a mesh axis runs over, the one named last changes fastest.
Arguments:
- image_raw: bfloat16 [16, 4096, 1152], P('dp', 'loop'), may hold values from -0.19921875 to 0.19921875
- text_feat: bfloat16 [16, 4096, 1152], P('dp', 'loop'), may hold values from -6 to 6
- text_head: bfloat16 [1152, 1152], replicated, may hold values from -0.1875 to 0.1875
- image_of_pair: int32 [16, 4096], P('dp', 'loop'), may hold values from 0 to 1023, as said below
- logit_scale: float32 [], replicated, may hold values from 10 to 30
- logit_bias: float32 [], replicated, may hold values from -3 to -1
Outputs:
- d_text_feat: float32 [16, 4096, 1152], P('dp', 'loop')
- d_image: float32 [32, 1024, 1152], P('loop', 'dp')
The draws below stay inside these ranges and needn't reach their ends.
Inputs may be any that keep to these rules, and one draw needn't show every extreme that they name: `image_of_pair`: pair row i of a replica belongs to column i // 128. Every image of a column is named by 1 to 5 pairs of that column over all replicas. Image m of a column is owned by the device of that column's loop index and dp index m // 64. The pairs of one device name images of one owner at most 20 times; in every draw some owner receives exactly 20 from every device of its column.
All inputs are finite; a program needn't handle non-finite values.
Results may differ from the reference program's by a relative error of at most 0.0057.
Values may be sent and summed in bfloat16 or wider, within the bound.
No kernel may reach another device: no remote copies, remote signals or barrier semaphores. Data moves between devices by JAX's collectives and lax.ppermute only.
A program may use at most 64 MiB of HBM per device.

```python
import math
import jax
import jax.numpy as jnp
from jax import lax

D = 1152
E = 1152
PAIR_DEV = 128
IMG_DEV = 64
REPLICAS = 16
COLUMNS = 32
ROWS = 4096
POOL = 1024
IMG_COL = 1024


def column_images(key):
    k_owner, k_heavy, k_light, k_first, k_second, k_device = jax.random.split(key, 6)
    heavy_owners = REPLICAS // 4
    quads = heavy_owners * IMG_DEV
    order = jax.random.permutation(k_owner, REPLICAS)
    owner_rank = jnp.argsort(order).astype(jnp.int32)
    heavy = jax.random.randint(k_heavy, (quads,), 3, 6)
    heavy = jnp.where(jnp.arange(quads) < IMG_DEV, 5, heavy).astype(jnp.int32)
    extra = 5 - heavy
    first = jax.random.randint(k_first, (quads,), 0, 3)
    second = jax.random.randint(k_second, (quads,), 0, 3)
    places = jnp.arange(3)[None, :]
    light = 1 + ((places == first[:, None]) & (extra[:, None] >= 1)).astype(jnp.int32)
    light = light + ((places == second[:, None]) & (extra[:, None] >= 2)).astype(jnp.int32)
    light_order = jax.random.permutation(k_light, 3 * quads)
    light_flat = light.reshape(-1)[light_order]
    images = jnp.arange(IMG_COL)
    rank = owner_rank[images // IMG_DEV]
    within = images % IMG_DEV
    heavy_index = jnp.clip(rank * IMG_DEV + within, 0, quads - 1)
    light_index = jnp.clip((rank - heavy_owners) * IMG_DEV + within, 0, 3 * quads - 1)
    counts = jnp.where(rank < heavy_owners, heavy[heavy_index], light_flat[light_index])
    ends = jnp.cumsum(counts)
    total = REPLICAS * PAIR_DEV
    caption = jnp.arange(total)
    image_of_caption = jnp.sum((ends[None, :] <= caption[:, None]).astype(jnp.int32), axis=1)
    sender = caption // 2 % REPLICAS
    slot = caption // (2 * REPLICAS) * 2 + caption % 2
    grid = jnp.zeros((REPLICAS, PAIR_DEV), jnp.int32).at[sender, slot].set(image_of_caption.astype(jnp.int32))
    device_keys = jax.random.split(k_device, REPLICAS)
    shuffles = jax.vmap(lambda k: jax.random.permutation(k, PAIR_DEV))(device_keys)
    return jnp.take_along_axis(grid, shuffles, axis=1)


def draw_image_of_pair(key, part):
    key = jax.random.fold_in(key, 11)
    column_keys = jax.random.split(key, COLUMNS)
    columns = jax.vmap(column_images)(column_keys)
    return jnp.transpose(columns, (1, 0, 2)).reshape(REPLICAS, ROWS).astype(jnp.int32)


def level_of(key, dims, cuts, least, largest):
    def one(axis_at, blocks):
        steps = jax.random.uniform(jax.random.fold_in(jax.random.fold_in(key, 6), axis_at), (blocks,), jnp.float32, least / len(cuts), largest / len(cuts))
        return jnp.repeat(jnp.exp(steps), dims[axis_at] // blocks).reshape((-1,) + (1,) * (len(dims) - axis_at - 1))

    loudness = one(*cuts[0])
    for cut in cuts[1:]:
        loudness = loudness * one(*cut)
    return loudness


def gaussian(key, dims, width, reach, cuts=(), kind=jnp.bfloat16):
    result = jax.random.normal(key, dims, jnp.float32) * width
    if len(cuts) > 0:
        result = level_of(key, dims, cuts, -0.22, 0.18) * result
    return jnp.clip(result, min=-reach, max=reach).astype(kind)


def setup_inputs(seed: int = 0) -> dict:
    splits = jax.random.split(jax.random.key(seed), 7)
    return {
        "image_raw": gaussian(splits[0], (REPLICAS, ROWS, E), 0.03, 0.19921875, ((0, 16), (1, 32))),
        "text_feat": gaussian(splits[1], (REPLICAS, ROWS, D), 1.0, 6.0, ((0, 16), (1, 32))),
        "text_head": gaussian(splits[2], (D, E), D ** -0.5, 0.1875),
        "image_of_pair": draw_image_of_pair(jax.random.fold_in(splits[6], 71), 0),
        "logit_scale": jnp.clip(jnp.exp(jax.random.uniform(splits[4], (), jnp.float32, math.log(10.0), math.log(30.0))), 10.0, 30.0),
        "logit_bias": jnp.clip(jax.random.uniform(splits[5], (), jnp.float32, -3.0, -1.0), -3.0, -1.0),
    }


EPS = 1e-06

def unit_rows(values):
    inv = lax.rsqrt(lax.optimization_barrier(jnp.sum(values * values, axis=-1, keepdims=True)) + EPS)
    return (values * inv, inv)

def reference(image_raw, text_feat, text_head, image_of_pair, logit_scale, logit_bias):
    unit_x, inv_x = unit_rows(image_raw.astype(jnp.float32))
    image_emb = unit_x.astype(jnp.bfloat16)
    text_pre = jnp.dot(text_feat.reshape(REPLICAS * ROWS, D), text_head, preferred_element_type=jnp.float32)
    unit_y, inv_y = unit_rows(text_pre.reshape(REPLICAS, ROWS, E))
    text_emb = unit_y.astype(jnp.bfloat16)
    pools_all = REPLICAS * (ROWS // POOL)
    column = jnp.arange(POOL, dtype=jnp.int32) // PAIR_DEV

    def pool_grads(items):
        x_block, y_block, labels = items
        same = (column[:, None] == column[None, :]) & (labels[:, None] == labels[None, :])
        logits = logit_scale * jnp.dot(x_block, y_block.T, preferred_element_type=jnp.float32) + logit_bias
        sign = jnp.where(same, jnp.float32(1.0), jnp.float32(-1.0))
        weight = (-sign * jax.nn.sigmoid(-sign * logits)).astype(jnp.bfloat16)
        d_img = logit_scale * jnp.dot(weight, y_block, preferred_element_type=jnp.float32)
        d_txt = logit_scale * jnp.dot(weight.T, x_block, preferred_element_type=jnp.float32)
        return (d_img, d_txt)
    d_img_emb, d_txt_emb = lax.map(pool_grads, (image_emb.reshape(pools_all, POOL, E), text_emb.reshape(pools_all, POOL, E), image_of_pair.reshape(pools_all, POOL)))
    d_img_emb = d_img_emb.reshape(REPLICAS, ROWS, E)
    d_txt_emb = d_txt_emb.reshape(REPLICAS, ROWS, E)
    d_image_pair = (d_img_emb - unit_x * lax.optimization_barrier(jnp.sum(unit_x * d_img_emb, axis=-1, keepdims=True))) * inv_x
    d_text_pre = ((d_txt_emb - unit_y * lax.optimization_barrier(jnp.sum(unit_y * d_txt_emb, axis=-1, keepdims=True))) * inv_y).astype(jnp.bfloat16)
    d_text_feat = jnp.dot(d_text_pre.reshape(REPLICAS * ROWS, E), text_head.T, preferred_element_type=jnp.float32)
    row_column = jnp.arange(ROWS, dtype=jnp.int32) // PAIR_DEV
    segment = (row_column[None, :] * IMG_COL + image_of_pair).astype(jnp.int32)
    d_image = jax.ops.segment_sum(d_image_pair.reshape(REPLICAS * ROWS, E), segment.reshape(-1), num_segments=COLUMNS * IMG_COL)
    return (d_text_feat.reshape(REPLICAS, ROWS, D), d_image.reshape(COLUMNS, IMG_COL, E))
```

```python
import functools

import jax
import jax.numpy as jnp
from jax import lax
from jax.experimental import pallas as pl
from jax.experimental.pallas import tpu as pltpu
from jax.sharding import PartitionSpec as P

EPS = 1e-06
IMG_DEV = 64
SLOTS = 20
MSG = 24
RING = 4
F32 = jnp.float32
BF16 = jnp.bfloat16


def call(kernel, outs, flops=0, bytes_accessed=0):
    return pl.pallas_call(
        kernel,
        out_shape=outs,
        compiler_params=pltpu.CompilerParams(vmem_limit_bytes=48 * 2**20),
        cost_estimate=pl.CostEstimate(flops=flops, bytes_accessed=bytes_accessed, transcendentals=0),
    )


def inv_norm(values):
    return lax.rsqrt(jnp.sum(values * values, axis=-1, keepdims=True) + EPS)


def dot(a, b, dims):
    return lax.dot_general(a, b, ((dims[0], dims[1]), ((), ())), preferred_element_type=F32)


NT = ((1,), (1,))
NN = ((1,), (0,))
TN = ((0,), (0,))


def embed_kernel(img_ref, feat_ref, head_ref, held_ref, unit_ref, inv_ref):
    x = img_ref[...].astype(F32)
    held_ref[0] = (x * inv_norm(x)).astype(BF16)
    pre = dot(feat_ref[...], head_ref[...], NN)
    inv = inv_norm(pre)
    unit = pre * inv
    held_ref[1] = unit.astype(BF16)
    unit_ref[...] = unit
    inv_ref[...] = inv


def text_kernel(feat_ref, head_ref, emb_ref):
    pre = dot(feat_ref[...], head_ref[...], NN)
    emb_ref[...] = (pre * inv_norm(pre)).astype(BF16)


def apart_weights(own, others, scale, shift):
    logits = scale * dot(own, others, NT) + shift
    return (1.0 / (1.0 + jnp.exp(-logits))).astype(BF16)


def near_kernel(
    scale_ref, shift_ref, lab_ref, labt_ref, held_ref, a_ref, b_ref, c_ref, img_ref, txt_ref
):
    scale, shift = scale_ref[0], shift_ref[0]
    x, y = held_ref[0], held_ref[1]
    same = labt_ref[...] == lab_ref[...]
    sign = jnp.where(same, F32(1.0), F32(-1.0))
    logits = scale * dot(x, y, NT) + shift
    home = (-sign / (1.0 + jnp.exp(sign * logits))).astype(BF16)
    others_y = jnp.concatenate([a_ref[1], b_ref[1], c_ref[1]], axis=0)
    img_ref[...] = dot(home, y, NN) + dot(apart_weights(x, others_y, scale, shift), others_y, NN)
    others_x = jnp.concatenate([a_ref[0], b_ref[0], c_ref[0]], axis=0)
    txt_ref[...] = dot(home, x, TN) + dot(apart_weights(y, others_x, scale, shift), others_x, NN)


def far_image_kernel(
    scale_ref, shift_ref, raw_ref, held_ref, part_ref, a_ref, b_ref, c_ref, d_ref, pick_ref, tag_ref, out_ref
):
    scale, shift = scale_ref[0], shift_ref[0]
    others = jnp.concatenate([a_ref[...], b_ref[...], c_ref[...], d_ref[...]], axis=0)
    weight = apart_weights(held_ref[0], others, scale, shift)
    grad = scale * (part_ref[...] + dot(weight, others, NN))
    x = raw_ref[...].astype(F32)
    inv = inv_norm(x)
    unit = x * inv
    pair = (grad - unit * jnp.sum(unit * grad, axis=-1, keepdims=True)) * inv
    rows = jnp.concatenate([pair.astype(BF16), tag_ref[...]], axis=0)
    sent = dot(pick_ref[...], rows, NN)
    for owner in range(out_ref.shape[0]):
        out_ref[owner] = sent[owner * MSG : (owner + 1) * MSG].astype(BF16)


def far_text_kernel(
    scale_ref, shift_ref, unit_ref, inv_ref, held_ref, part_ref, a_ref, b_ref, c_ref, d_ref, head_ref, out_ref
):
    scale, shift = scale_ref[0], shift_ref[0]
    others = jnp.concatenate([a_ref[...], b_ref[...], c_ref[...], d_ref[...]], axis=0)
    weight = apart_weights(held_ref[1], others, scale, shift)
    grad = scale * (part_ref[...] + dot(weight, others, NN))
    unit = unit_ref[...]
    pre = (grad - unit * jnp.sum(unit * grad, axis=-1, keepdims=True)) * inv_ref[...]
    out_ref[...] = dot(pre.astype(BF16), head_ref[...], NT)


def sum_kernel(arrived_ref, out_ref):
    image = lax.broadcasted_iota(jnp.int32, (IMG_DEV, MSG), 0).astype(F32) + 1.0
    total = jnp.zeros(out_ref.shape, F32)
    for sender in range(arrived_ref.shape[0]):
        rows = arrived_ref[sender]
        tags = rows.astype(F32)[SLOTS : SLOTS + 1, :MSG]
        total = total + dot((image == tags).astype(BF16), rows, NN)
    out_ref[...] = total


def routing(labels, owners, width):
    count = labels.shape[0]
    owner = labels // IMG_DEV
    index = jnp.arange(count)
    rank = jnp.sum(
        ((owner[:, None] == owner[None, :]) & (index[None, :] < index[:, None])).astype(jnp.int32), axis=1
    )
    slot = owner * MSG + rank
    row = jnp.arange(owners * MSG)
    pick = row[:, None] == slot[None, :]
    mark = row[:, None] == (index * MSG + SLOTS)[None, :]
    picks = jnp.concatenate([pick, mark], axis=1).astype(BF16)
    mine = (index[:, None] == owner[None, :]).astype(BF16)
    values = jnp.where(
        rank[:, None] == jnp.arange(width)[None, :], (labels % IMG_DEV + 1)[:, None], 0
    ).astype(BF16)
    tags = jnp.dot(mine, values, preferred_element_type=F32).astype(BF16)
    return picks, tags


def shards(image_raw, text_feat, text_head, image_of_pair, logit_scale, logit_bias):
    rows, width = image_raw.shape[1:]
    owners = lax.axis_size("dp")
    loops = lax.axis_size("loop")
    image, feat, labels = image_raw[0], text_feat[0], image_of_pair[0]
    scale, shift = logit_scale[None], logit_bias[None]
    across = [(i, i ^ RING) for i in range(loops)]
    turns = [
        [(i, i & ~(RING - 1) | (i + 1) % RING) for i in range(loops)],
        [(i, i & ~(RING - 1) | (i - 1) % RING) for i in range(loops)],
        [(i, i ^ 2) for i in range(loops)],
    ]

    def ring(value):
        return [lax.ppermute(value, "loop", turn) for turn in turns]

    block = jax.ShapeDtypeStruct((rows, width), BF16)
    wide = jax.ShapeDtypeStruct((rows, width), F32)
    smem = pl.BlockSpec(memory_space=pltpu.SMEM)

    far_feat = lax.ppermute(feat, "loop", across)
    held, unit_y, inv_y = call(
        embed_kernel,
        (
            jax.ShapeDtypeStruct((2, rows, width), BF16),
            wide,
            jax.ShapeDtypeStruct((rows, 1), F32),
        ),
    )(image, feat, text_head)
    near = ring(held)
    image_emb = held[0]
    image_emb, far_feat = lax.optimization_barrier((image_emb, far_feat))
    far_x = lax.ppermute(image_emb, "loop", across)
    far_y = call(text_kernel, block)(far_feat, text_head)
    far_ys = [far_y, *ring(far_y)]
    scalars = functools.partial(with_scalars, scale, shift)
    part_img, part_txt = scalars(near_kernel, (wide, wide), labels[None, :], labels[:, None], held, *near)
    picks, tags = routing(labels, owners, width)
    sent = scalars(
        far_image_kernel,
        jax.ShapeDtypeStruct((owners, MSG, width), BF16),
        image, held, part_img, *far_ys, picks, tags,
    )
    arrived = lax.all_to_all(sent, "dp", split_axis=0, concat_axis=0, tiled=True)
    far_xs = [far_x, *ring(far_x)]
    d_text_feat = scalars(far_text_kernel, wide, unit_y, inv_y, held, part_txt, *far_xs, text_head)
    d_image = call(sum_kernel, jax.ShapeDtypeStruct((IMG_DEV, width), F32))(arrived)
    return (d_text_feat[None], d_image[None])


def with_scalars(scale, shift, kernel, outs, *operands):
    smem = pl.BlockSpec(memory_space=pltpu.SMEM)
    vmem = pl.BlockSpec(memory_space=pltpu.VMEM)
    return pl.pallas_call(
        kernel,
        out_shape=outs,
        in_specs=[smem, smem] + [vmem] * len(operands),
        compiler_params=pltpu.CompilerParams(vmem_limit_bytes=48 * 2**20),
    )(scale, shift, *operands)


def solution(mesh):
    placed = (P("dp", "loop", None), P("dp", "loop", None), P(), P("dp", "loop"), P(), P())
    return jax.shard_map(
        shards,
        mesh=mesh,
        in_specs=placed,
        out_specs=(P("dp", "loop", None), P("loop", "dp", None)),
        check_vma=False,
    )
```

```python
import jax
import jax.numpy as jnp
from jax import lax
from jax.experimental import pallas as pl
from jax.experimental.pallas import tpu as pltpu
from jax.sharding import PartitionSpec as P

EPS = 1e-06
IMG_DEV = 64
RING = 4
LANES = 128
MAIN = 16
EXTRA = 4
F32 = jnp.float32
BF16 = jnp.bfloat16

NT = ((1,), (1,))
NN = ((1,), (0,))
TN = ((0,), (0,))


def call(kernel, outs, *operands, scalars=0, scratch=()):
    smem = pl.BlockSpec(memory_space=pltpu.SMEM)
    vmem = pl.BlockSpec(memory_space=pltpu.VMEM)
    return pl.pallas_call(
        kernel,
        out_shape=outs,
        in_specs=[smem] * scalars + [vmem] * (len(operands) - scalars),
        scratch_shapes=scratch,
        compiler_params=pltpu.CompilerParams(vmem_limit_bytes=48 * 2**20),
    )(*operands)


def inv_norm(values):
    return lax.rsqrt(jnp.sum(values * values, axis=-1, keepdims=True) + EPS)


def dot(a, b, dims):
    return lax.dot_general(a, b, (dims, ((), ())), preferred_element_type=F32)


def embed_kernel(img_ref, feat_ref, head_ref, x_ref, y_ref, unit_ref, inv_ref):
    x = img_ref[...].astype(F32)
    x_ref[...] = (x * inv_norm(x)).astype(BF16)
    pre = dot(feat_ref[...], head_ref[...], NN)
    inv = inv_norm(pre)
    unit = pre * inv
    y_ref[...] = unit.astype(BF16)
    unit_ref[...] = unit
    inv_ref[...] = inv


def text_kernel(feat_ref, head_ref, emb_ref):
    pre = dot(feat_ref[...], head_ref[...], NN)
    emb_ref[...] = (pre * inv_norm(pre)).astype(BF16)


def apart_weights(own, others, scale, shift):
    logits = scale * dot(own, others, NT) + shift
    return (1.0 / (1.0 + jnp.exp(-logits))).astype(BF16)


def column(row):
    size = row.shape[1]
    at = [lax.broadcasted_iota(jnp.int32, (size, size), axis) for axis in range(2)]
    return jnp.sum(jnp.where(at[0] == at[1], row, 0), axis=1, keepdims=True)


def home_weights(x, y, lab_ref, scale, shift):
    lab = lab_ref[...]
    sign = jnp.where(column(lab) == lab, F32(1.0), F32(-1.0))
    logits = scale * dot(x, y, NT) + shift
    return (-sign / (1.0 + jnp.exp(sign * logits))).astype(BF16)


def near_image_kernel(scale_ref, shift_ref, lab_ref, x_ref, y_ref, a_ref, b_ref, c_ref, out_ref):
    scale, shift = scale_ref[0], shift_ref[0]
    x, y = x_ref[...], y_ref[...]
    home = home_weights(x, y, lab_ref, scale, shift)
    others = jnp.concatenate([a_ref[...], b_ref[...], c_ref[...]], axis=0)
    out_ref[...] = dot(home, y, NN) + dot(apart_weights(x, others, scale, shift), others, NN)


def far_image_kernel(
    scale_ref, shift_ref, raw_ref, x_ref, part_ref, a_ref, b_ref, c_ref, d_ref, pick_ref, tag_ref, out_ref
):
    scale, shift = scale_ref[0], shift_ref[0]
    others = jnp.concatenate([a_ref[...], b_ref[...], c_ref[...], d_ref[...]], axis=0)
    weight = apart_weights(x_ref[...], others, scale, shift)
    grad = scale * (part_ref[...] + dot(weight, others, NN))
    x = raw_ref[...].astype(F32)
    inv = inv_norm(x)
    unit = x * inv
    pair = (grad - unit * jnp.sum(unit * grad, axis=-1, keepdims=True)) * inv
    sent = dot(pick_ref[...], pair.astype(BF16), NN)
    low = lax.broadcasted_iota(jnp.int32, (2 * EXTRA, LANES), 0) < EXTRA
    step = MAIN + 2 * EXTRA
    for owner in range(out_ref.shape[0]):
        rows = sent[owner * step : (owner + 1) * step]
        cols = [rows[:, at : at + LANES] for at in range(0, rows.shape[1], LANES)]
        ends = [col[MAIN:] for col in cols] + [tag_ref[owner]]
        pairs = [jnp.where(low, ends[at], ends[at + 1]) for at in range(0, len(ends), 2)]
        out_ref[owner] = jnp.concatenate([col[:MAIN] for col in cols] + pairs, axis=0).astype(BF16)


def text_grad_kernel(scale_ref, shift_ref, lab_ref, unit_ref, inv_ref, x_ref, y_ref, *refs):
    *other_refs, head_ref, out_ref = refs
    scale, shift = scale_ref[0], shift_ref[0]
    x, y = x_ref[...], y_ref[...]
    home = home_weights(x, y, lab_ref, scale, shift)
    others = jnp.concatenate([ref[...] for ref in other_refs], axis=0)
    weight = apart_weights(y, others, scale, shift)
    grad = scale * (dot(home, x, TN) + dot(weight, others, NN))
    unit = unit_ref[...]
    pre = (grad - unit * jnp.sum(unit * grad, axis=-1, keepdims=True)) * inv_ref[...]
    out_ref[...] = dot(pre.astype(BF16), head_ref[...], NT)


def sum_kernel(arrived_ref, out_ref, main_ref):
    senders = arrived_ref.shape[0]
    chunks = out_ref.shape[1] // LANES
    ends = []
    for sender in range(senders):
        block = arrived_ref[sender]
        for c in range(chunks):
            main_ref[sender * MAIN : (sender + 1) * MAIN, c * LANES : (c + 1) * LANES] = block[
                c * MAIN : (c + 1) * MAIN
            ]
        tail = block.astype(F32)[chunks * MAIN :]
        ends.append([tail[at : at + 2 * EXTRA] for at in range(0, tail.shape[0], 2 * EXTRA)])
    image = lax.broadcasted_iota(jnp.int32, (IMG_DEV, LANES), 0).astype(F32) + 1.0
    half = senders // 2
    first = sum(end[-1] for end in ends[:half])
    second = sum(end[-1] for end in ends[half:])
    both = first + second
    match = jnp.concatenate(
        [image == first[EXTRA : EXTRA + 1], image == second[EXTRA : EXTRA + 1]], axis=1
    ).astype(BF16)
    low = lax.broadcasted_iota(jnp.int32, (IMG_DEV, LANES), 1) % (2 * EXTRA) < EXTRA
    extra = image == both[EXTRA + 1 : EXTRA + 2]
    extras = ((extra & low).astype(BF16), (extra & ~low).astype(BF16))
    total = dot(match, main_ref[...], NN)
    for c in range(chunks):
        tail = jnp.concatenate([end[c // 2] for end in ends], axis=0).astype(BF16)
        out_ref[:, c * LANES : (c + 1) * LANES] = total[:, c * LANES : (c + 1) * LANES] + dot(
            extras[c % 2], tail, NN
        )


def routing_kernel(me_ref, lab_ref, pick_ref, tag_ref):
    me = me_ref[0]
    row = lab_ref[...]
    count = row.shape[1]
    owners = tag_ref.shape[0]
    col = column(row)
    owner_row, owner_col = row // IMG_DEV, col // IMG_DEV
    at = [lax.broadcasted_iota(jnp.int32, (count, count), axis) for axis in range(2)]
    same = owner_col == owner_row
    rank_row = jnp.sum(jnp.where(same & (at[0] < at[1]), 1, 0), axis=0, keepdims=True)
    rank_col = jnp.sum(jnp.where(same & (at[1] < at[0]), 1, 0), axis=1, keepdims=True)
    step = MAIN + 2 * EXTRA
    slot = lax.broadcasted_iota(jnp.int32, (step, count), 0)
    want = jnp.where(slot < MAIN, slot, MAIN + slot % EXTRA)
    hit = want == rank_row
    picks = [jnp.where(hit & (owner_row == owner), F32(1.0), F32(0.0)) for owner in range(owners)]
    pick_ref[...] = jnp.concatenate(picks, axis=0).astype(BF16)
    lane = at[1]
    value = (col % IMG_DEV + 1).astype(F32)
    main_at = (rank_col < MAIN) & (lane - me % (owners // 2) * MAIN == rank_col)
    extra_at = (lane // (2 * EXTRA) == me) & (MAIN + lane % EXTRA == rank_col)
    marks = jnp.concatenate([jnp.where(main_at, value, 0.0), jnp.where(extra_at, value, 0.0)], axis=1)
    mine = lax.broadcasted_iota(jnp.int32, (owners, count), 0) == owner_row
    tags = dot(jnp.where(mine, F32(1.0), F32(0.0)).astype(BF16), marks.astype(BF16), NN)
    sub = lax.broadcasted_iota(jnp.int32, (2 * EXTRA, LANES), 0)
    for owner in range(owners):
        main, extra = tags[owner : owner + 1, :LANES], tags[owner : owner + 1, LANES:]
        tag_ref[owner] = jnp.where(sub == EXTRA, main, jnp.where(sub == EXTRA + 1, extra, 0.0))


def shards(image_raw, text_feat, text_head, image_of_pair, logit_scale, logit_bias):
    rows, width = image_raw.shape[1:]
    owners = lax.axis_size("dp")
    loops = lax.axis_size("loop")
    image, feat, labels = image_raw[0], text_feat[0], image_of_pair[0]
    scalars = (logit_scale[None], logit_bias[None])
    lab = labels[None, :]
    across = [(i, i ^ RING) for i in range(loops)]
    turns = [
        [(i, i & ~(RING - 1) | (i + 1) % RING) for i in range(loops)],
        [(i, i & ~(RING - 1) | (i - 1) % RING) for i in range(loops)],
        [(i, i ^ 2) for i in range(loops)],
    ]

    def ring(value):
        return [lax.ppermute(value, "loop", turn) for turn in turns]

    block = jax.ShapeDtypeStruct((rows, width), BF16)
    wide = jax.ShapeDtypeStruct((rows, width), F32)

    step = MAIN + 2 * EXTRA
    halves = [list(range(at, at + RING)) for at in range(0, loops, RING)]
    picks, tags = call(
        routing_kernel,
        (
            jax.ShapeDtypeStruct((owners * step, rows), BF16),
            jax.ShapeDtypeStruct((owners, 2 * EXTRA, LANES), F32),
        ),
        lax.axis_index("dp")[None], lab, scalars=1,
    )
    far_feat = lax.ppermute(feat, "loop", across)
    x, y, unit_y, inv_y = call(
        embed_kernel, (block, block, wide, jax.ShapeDtypeStruct((rows, 1), F32)), image, feat, text_head
    )
    part = call(near_image_kernel, wide, *scalars, lab, x, y, *ring(y), scalars=2)
    x_out, far_feat = lax.optimization_barrier((x, far_feat))
    far_x = lax.ppermute(x_out, "loop", across)
    far_y = call(text_kernel, block, far_feat, text_head)
    far_ys = ring(far_y)
    part, far_x = lax.optimization_barrier((part, far_x))
    sent = call(
        far_image_kernel,
        jax.ShapeDtypeStruct((owners, (MAIN + EXTRA) * width // LANES + EXTRA, LANES), BF16),
        *scalars, image, x, part, far_y, *far_ys, picks, tags, scalars=2,
    )
    sent, x_near = lax.optimization_barrier((sent, x))
    arrived = lax.all_to_all(sent, "dp", split_axis=0, concat_axis=0, tiled=True)
    xs = [*ring(x_near), far_x, *ring(far_x)]
    d_text_feat = call(
        text_grad_kernel, wide, *scalars, lab, unit_y, inv_y, x, y, *xs, text_head, scalars=2
    )
    d_image = call(
        sum_kernel,
        jax.ShapeDtypeStruct((IMG_DEV, width), F32),
        arrived,
        scratch=[pltpu.VMEM((owners * MAIN, width), BF16)],
    )
    return (d_text_feat[None], d_image[None])


def solution(mesh):
    placed = (P("dp", "loop", None), P("dp", "loop", None), P(), P("dp", "loop"), P(), P())
    return jax.shard_map(
        shards,
        mesh=mesh,
        in_specs=placed,
        out_specs=(P("dp", "loop", None), P("loop", "dp", None)),
        check_vma=False,
    )
```

```python
import jax
import jax.numpy as jnp
from jax import lax
from jax.experimental import pallas as pl
from jax.experimental.pallas import tpu as pltpu
from jax.sharding import PartitionSpec as P

EPS = 1e-06
IMG_DEV = 64
RING = 4
LANES = 128
MAIN = 16
EXTRA = 4
F32 = jnp.float32
BF16 = jnp.bfloat16

NT = ((1,), (1,))
NN = ((1,), (0,))
TN = ((0,), (0,))


def call(kernel, outs, *operands, scalars=0, scratch=()):
    smem = pl.BlockSpec(memory_space=pltpu.SMEM)
    vmem = pl.BlockSpec(memory_space=pltpu.VMEM)
    return pl.pallas_call(
        kernel,
        out_shape=outs,
        in_specs=[smem] * scalars + [vmem] * (len(operands) - scalars),
        scratch_shapes=scratch,
        compiler_params=pltpu.CompilerParams(vmem_limit_bytes=48 * 2**20),
    )(*operands)


def inv_norm(values):
    return lax.rsqrt(jnp.sum(values * values, axis=-1, keepdims=True) + EPS)


def dot(a, b, dims):
    return lax.dot_general(a, b, (dims, ((), ())), preferred_element_type=F32)


def embed_kernel(img_ref, feat_ref, head_ref, x_ref, y_ref, unit_ref, inv_ref):
    x = img_ref[...].astype(F32)
    x_ref[...] = (x * inv_norm(x)).astype(BF16)
    pre = dot(feat_ref[...], head_ref[...], NN)
    inv = inv_norm(pre)
    unit = pre * inv
    y_ref[...] = unit.astype(BF16)
    unit_ref[...] = unit
    inv_ref[...] = inv


def text_kernel(feat_ref, head_ref, emb_ref):
    pre = dot(feat_ref[...], head_ref[...], NN)
    emb_ref[...] = (pre * inv_norm(pre)).astype(BF16)


def apart_weights(own, others, scale, shift):
    logits = scale * dot(own, others, NT) + shift
    return (1.0 / (1.0 + jnp.exp(-logits))).astype(BF16)


def column(row):
    size = row.shape[1]
    at = [lax.broadcasted_iota(jnp.int32, (size, size), axis) for axis in range(2)]
    return jnp.sum(jnp.where(at[0] == at[1], row, 0), axis=1, keepdims=True)


def home_weights(x, y, lab_ref, scale, shift):
    lab = lab_ref[...]
    sign = jnp.where(column(lab) == lab, F32(1.0), F32(-1.0))
    logits = scale * dot(x, y, NT) + shift
    return (-sign / (1.0 + jnp.exp(sign * logits))).astype(BF16)


def near_image_kernel(scale_ref, shift_ref, lab_ref, x_ref, y_ref, a_ref, b_ref, c_ref, out_ref):
    scale, shift = scale_ref[0], shift_ref[0]
    x, y = x_ref[...], y_ref[...]
    home = home_weights(x, y, lab_ref, scale, shift)
    others = jnp.concatenate([a_ref[...], b_ref[...], c_ref[...]], axis=0)
    out_ref[...] = dot(home, y, NN) + dot(apart_weights(x, others, scale, shift), others, NN)


def far_image_kernel(
    scale_ref, shift_ref, raw_ref, x_ref, part_ref, a_ref, b_ref, c_ref, d_ref, pick_ref, tag_ref, out_ref
):
    scale, shift = scale_ref[0], shift_ref[0]
    others = jnp.concatenate([a_ref[...], b_ref[...], c_ref[...], d_ref[...]], axis=0)
    weight = apart_weights(x_ref[...], others, scale, shift)
    grad = scale * (part_ref[...] + dot(weight, others, NN))
    x = raw_ref[...].astype(F32)
    inv = inv_norm(x)
    unit = x * inv
    pair = (grad - unit * jnp.sum(unit * grad, axis=-1, keepdims=True)) * inv
    sent = dot(pick_ref[...], pair.astype(BF16), NN)
    low = lax.broadcasted_iota(jnp.int32, (2 * EXTRA, LANES), 0) < EXTRA
    step = MAIN + 2 * EXTRA
    for owner in range(out_ref.shape[0]):
        rows = sent[owner * step : (owner + 1) * step]
        cols = [rows[:, at : at + LANES] for at in range(0, rows.shape[1], LANES)]
        ends = [col[MAIN:] for col in cols] + [tag_ref[owner]]
        pairs = [jnp.where(low, ends[at], ends[at + 1]) for at in range(0, len(ends), 2)]
        out_ref[owner] = jnp.concatenate([col[:MAIN] for col in cols] + pairs, axis=0).astype(BF16)


def text_grad_kernel(scale_ref, shift_ref, lab_ref, unit_ref, inv_ref, x_ref, y_ref, *refs):
    *other_refs, head_ref, out_ref = refs
    scale, shift = scale_ref[0], shift_ref[0]
    x, y = x_ref[...], y_ref[...]
    home = home_weights(x, y, lab_ref, scale, shift)
    others = jnp.concatenate([ref[...] for ref in other_refs], axis=0)
    weight = apart_weights(y, others, scale, shift)
    grad = scale * (dot(home, x, TN) + dot(weight, others, NN))
    unit = unit_ref[...]
    pre = (grad - unit * jnp.sum(unit * grad, axis=-1, keepdims=True)) * inv_ref[...]
    out_ref[...] = dot(pre.astype(BF16), head_ref[...], NT)


def sum_kernel(arrived_ref, out_ref, main_ref):
    senders = arrived_ref.shape[0]
    chunks = out_ref.shape[1] // LANES
    ends = []
    for sender in range(senders):
        block = arrived_ref[sender]
        for c in range(chunks):
            main_ref[sender * MAIN : (sender + 1) * MAIN, c * LANES : (c + 1) * LANES] = block[
                c * MAIN : (c + 1) * MAIN
            ]
        tail = block.astype(F32)[chunks * MAIN :]
        ends.append([tail[at : at + 2 * EXTRA] for at in range(0, tail.shape[0], 2 * EXTRA)])
    image = lax.broadcasted_iota(jnp.int32, (IMG_DEV, LANES), 0).astype(F32) + 1.0
    half = senders // 2
    first = sum(end[-1] for end in ends[:half])
    second = sum(end[-1] for end in ends[half:])
    both = first + second
    match = jnp.concatenate(
        [image == first[EXTRA : EXTRA + 1], image == second[EXTRA : EXTRA + 1]], axis=1
    ).astype(BF16)
    low = lax.broadcasted_iota(jnp.int32, (IMG_DEV, LANES), 1) % (2 * EXTRA) < EXTRA
    extra = image == both[EXTRA + 1 : EXTRA + 2]
    extras = ((extra & low).astype(BF16), (extra & ~low).astype(BF16))
    total = dot(match, main_ref[...], NN)
    for c in range(chunks):
        tail = jnp.concatenate([end[c // 2] for end in ends], axis=0).astype(BF16)
        out_ref[:, c * LANES : (c + 1) * LANES] = total[:, c * LANES : (c + 1) * LANES] + dot(
            extras[c % 2], tail, NN
        )


def routing_kernel(me_ref, lab_ref, pick_ref, tag_ref):
    me = me_ref[0]
    row = lab_ref[...]
    count = row.shape[1]
    owners = tag_ref.shape[0]
    col = column(row)
    owner_row, owner_col = row // IMG_DEV, col // IMG_DEV
    at = [lax.broadcasted_iota(jnp.int32, (count, count), axis) for axis in range(2)]
    same = owner_col == owner_row
    rank_row = jnp.sum(jnp.where(same & (at[0] < at[1]), 1, 0), axis=0, keepdims=True)
    rank_col = jnp.sum(jnp.where(same & (at[1] < at[0]), 1, 0), axis=1, keepdims=True)
    step = MAIN + 2 * EXTRA
    slot = lax.broadcasted_iota(jnp.int32, (step, count), 0)
    want = jnp.where(slot < MAIN, slot, MAIN + slot % EXTRA)
    hit = want == rank_row
    picks = [jnp.where(hit & (owner_row == owner), F32(1.0), F32(0.0)) for owner in range(owners)]
    pick_ref[...] = jnp.concatenate(picks, axis=0).astype(BF16)
    lane = at[1]
    value = (col % IMG_DEV + 1).astype(F32)
    main_at = (rank_col < MAIN) & (lane - me % (owners // 2) * MAIN == rank_col)
    extra_at = (lane // (2 * EXTRA) == me) & (MAIN + lane % EXTRA == rank_col)
    marks = jnp.concatenate([jnp.where(main_at, value, 0.0), jnp.where(extra_at, value, 0.0)], axis=1)
    mine = lax.broadcasted_iota(jnp.int32, (owners, count), 0) == owner_row
    tags = dot(jnp.where(mine, F32(1.0), F32(0.0)).astype(BF16), marks.astype(BF16), NN)
    sub = lax.broadcasted_iota(jnp.int32, (2 * EXTRA, LANES), 0)
    for owner in range(owners):
        main, extra = tags[owner : owner + 1, :LANES], tags[owner : owner + 1, LANES:]
        tag_ref[owner] = jnp.where(sub == EXTRA, main, jnp.where(sub == EXTRA + 1, extra, 0.0))


def shards(image_raw, text_feat, text_head, image_of_pair, logit_scale, logit_bias):
    rows, width = image_raw.shape[1:]
    owners = lax.axis_size("dp")
    loops = lax.axis_size("loop")
    image, feat, labels = image_raw[0], text_feat[0], image_of_pair[0]
    scalars = (logit_scale[None], logit_bias[None])
    lab = labels[None, :]
    across = [(i, i ^ RING) for i in range(loops)]
    turns = [
        [(i, i & ~(RING - 1) | (i + 1) % RING) for i in range(loops)],
        [(i, i & ~(RING - 1) | (i - 1) % RING) for i in range(loops)],
        [(i, i ^ 2) for i in range(loops)],
    ]

    def ring(value):
        return [lax.ppermute(value, "loop", turn) for turn in turns]

    block = jax.ShapeDtypeStruct((rows, width), BF16)
    wide = jax.ShapeDtypeStruct((rows, width), F32)

    step = MAIN + 2 * EXTRA
    halves = [list(range(at, at + RING)) for at in range(0, loops, RING)]
    picks, tags = call(
        routing_kernel,
        (
            jax.ShapeDtypeStruct((owners * step, rows), BF16),
            jax.ShapeDtypeStruct((owners, 2 * EXTRA, LANES), F32),
        ),
        lax.axis_index("dp")[None], lab, scalars=1,
    )
    far_feat = lax.ppermute(feat, "loop", across)
    x, y, unit_y, inv_y = call(
        embed_kernel, (block, block, wide, jax.ShapeDtypeStruct((rows, 1), F32)), image, feat, text_head
    )
    part = call(near_image_kernel, wide, *scalars, lab, x, y, *ring(y), scalars=2)
    far_x = lax.ppermute(x, "loop", across)
    far_y = call(text_kernel, block, far_feat, text_head)
    far_ys = ring(far_y)
    part, far_x = lax.optimization_barrier((part, far_x))
    sent = call(
        far_image_kernel,
        jax.ShapeDtypeStruct((owners, (MAIN + EXTRA) * width // LANES + EXTRA, LANES), BF16),
        *scalars, image, x, part, far_y, *far_ys, picks, tags, scalars=2,
    )
    sent, x_near = lax.optimization_barrier((sent, x))
    arrived = lax.all_to_all(sent, "dp", split_axis=0, concat_axis=0, tiled=True)
    xs = [*ring(x_near), far_x, *ring(far_x)]
    d_text_feat = call(
        text_grad_kernel, wide, *scalars, lab, unit_y, inv_y, x, y, *xs, text_head, scalars=2
    )
    d_image = call(
        sum_kernel,
        jax.ShapeDtypeStruct((IMG_DEV, width), F32),
        arrived,
        scratch=[pltpu.VMEM((owners * MAIN, width), BF16)],
    )
    return (d_text_feat[None], d_image[None])


def solution(mesh):
    placed = (P("dp", "loop", None), P("dp", "loop", None), P(), P("dp", "loop"), P(), P())
    return jax.shard_map(
        shards,
        mesh=mesh,
        in_specs=placed,
        out_specs=(P("dp", "loop", None), P("loop", "dp", None)),
        check_vma=False,
    )
```

```python
import jax
import jax.numpy as jnp
from jax import lax
from jax.experimental import pallas as pl
from jax.experimental.pallas import tpu as pltpu
from jax.sharding import PartitionSpec as P

EPS = 1e-06
IMG_DEV = 64
RING = 4
LANES = 128
MAIN = 16
EXTRA = 4
F32 = jnp.float32
BF16 = jnp.bfloat16

NT = ((1,), (1,))
NN = ((1,), (0,))
TN = ((0,), (0,))


def call(kernel, outs, *operands, scalars=0, away=0, scratch=()):
    smem = pl.BlockSpec(memory_space=pltpu.SMEM)
    vmem = pl.BlockSpec(memory_space=pltpu.VMEM)
    return pl.pallas_call(
        kernel,
        out_shape=outs,
        in_specs=[smem] * scalars
        + [vmem] * (len(operands) - scalars - away)
        + [pl.BlockSpec(memory_space=pl.ANY)] * away,
        scratch_shapes=scratch,
        compiler_params=pltpu.CompilerParams(vmem_limit_bytes=48 * 2**20),
    )(*operands)


def inv_norm(values):
    return lax.rsqrt(jnp.sum(values * values, axis=-1, keepdims=True) + EPS)


def dot(a, b, dims):
    return lax.dot_general(a, b, (dims, ((), ())), preferred_element_type=F32)


def embed_kernel(img_ref, feat_ref, head_ref, x_ref, y_ref, unit_ref, inv_ref):
    x = img_ref[...].astype(F32)
    x_ref[...] = (x * inv_norm(x)).astype(BF16)
    pre = dot(feat_ref[...], head_ref[...], NN)
    inv = inv_norm(pre)
    unit = pre * inv
    y_ref[...] = unit.astype(BF16)
    unit_ref[...] = unit
    inv_ref[...] = inv


def text_kernel(feat_ref, head_ref, emb_ref):
    pre = dot(feat_ref[...], head_ref[...], NN)
    emb_ref[...] = (pre * inv_norm(pre)).astype(BF16)


def apart_weights(own, others, scale, shift):
    logits = scale * dot(own, others, NT) + shift
    return (1.0 / (1.0 + jnp.exp(-logits))).astype(BF16)


def column(row):
    size = row.shape[1]
    at = [lax.broadcasted_iota(jnp.int32, (size, size), axis) for axis in range(2)]
    return jnp.sum(jnp.where(at[0] == at[1], row, 0), axis=1, keepdims=True)


def home_weights(x, y, lab_ref, scale, shift):
    lab = lab_ref[...]
    sign = jnp.where(column(lab) == lab, F32(1.0), F32(-1.0))
    logits = scale * dot(x, y, NT) + shift
    return (-sign / (1.0 + jnp.exp(sign * logits))).astype(BF16)


def near_image_kernel(scale_ref, shift_ref, lab_ref, x_ref, y_ref, a_ref, b_ref, c_ref, out_ref):
    scale, shift = scale_ref[0], shift_ref[0]
    x, y = x_ref[...], y_ref[...]
    home = home_weights(x, y, lab_ref, scale, shift)
    others = jnp.concatenate([a_ref[...], b_ref[...], c_ref[...]], axis=0)
    out_ref[...] = dot(home, y, NN) + dot(apart_weights(x, others, scale, shift), others, NN)


def far_image_kernel(
    scale_ref, shift_ref, raw_ref, x_ref, part_ref, a_ref, b_ref, c_ref, d_ref, pick_ref, tag_ref, out_ref
):
    scale, shift = scale_ref[0], shift_ref[0]
    others = jnp.concatenate([a_ref[...], b_ref[...], c_ref[...], d_ref[...]], axis=0)
    weight = apart_weights(x_ref[...], others, scale, shift)
    grad = scale * (part_ref[...] + dot(weight, others, NN))
    x = raw_ref[...].astype(F32)
    inv = inv_norm(x)
    unit = x * inv
    pair = (grad - unit * jnp.sum(unit * grad, axis=-1, keepdims=True)) * inv
    sent = dot(pick_ref[...], pair.astype(BF16), NN)
    low = lax.broadcasted_iota(jnp.int32, (2 * EXTRA, LANES), 0) < EXTRA
    step = MAIN + 2 * EXTRA
    for owner in range(out_ref.shape[0]):
        rows = sent[owner * step : (owner + 1) * step]
        cols = [rows[:, at : at + LANES] for at in range(0, rows.shape[1], LANES)]
        ends = [col[MAIN:] for col in cols] + [tag_ref[owner]]
        pairs = [jnp.where(low, ends[at], ends[at + 1]) for at in range(0, len(ends), 2)]
        out_ref[owner] = jnp.concatenate([col[:MAIN] for col in cols] + pairs, axis=0).astype(BF16)


def near_text_kernel(scale_ref, shift_ref, lab_ref, x_ref, y_ref, a_ref, b_ref, c_ref, d_ref, out_ref):
    scale, shift = scale_ref[0], shift_ref[0]
    x, y = x_ref[...], y_ref[...]
    home = home_weights(x, y, lab_ref, scale, shift)
    others = jnp.concatenate([a_ref[...], b_ref[...], c_ref[...], d_ref[...]], axis=0)
    out_ref[...] = dot(home, x, TN) + dot(apart_weights(y, others, scale, shift), others, NN)


def text_grad_kernel(
    scale_ref, shift_ref, y_ref, part_ref, a_ref, b_ref, c_ref, inv_hbm, unit_hbm, head_hbm, out_ref,
    inv_ref, unit_ref, head_ref, sems,
):
    scale, shift = scale_ref[0], shift_ref[0]
    pairs = ((inv_hbm, inv_ref), (unit_hbm, unit_ref), (head_hbm, head_ref))
    copies = [pltpu.make_async_copy(src, dst, sems.at[at]) for at, (src, dst) in enumerate(pairs)]
    for copy in copies:
        copy.start()
    others = jnp.concatenate([a_ref[...], b_ref[...], c_ref[...]], axis=0)
    weight = apart_weights(y_ref[...], others, scale, shift)
    grad = scale * (part_ref[...] + dot(weight, others, NN))
    copies[0].wait()
    copies[1].wait()
    unit = unit_ref[...]
    pre = (grad - unit * jnp.sum(unit * grad, axis=-1, keepdims=True)) * inv_ref[...]
    copies[2].wait()
    out_ref[...] = dot(pre.astype(BF16), head_ref[...], NT)


def sum_kernel(arrived_ref, out_ref, main_ref):
    senders = arrived_ref.shape[0]
    chunks = out_ref.shape[1] // LANES
    ends = []
    for sender in range(senders):
        block = arrived_ref[sender]
        for c in range(chunks):
            main_ref[sender * MAIN : (sender + 1) * MAIN, c * LANES : (c + 1) * LANES] = block[
                c * MAIN : (c + 1) * MAIN
            ]
        tail = block.astype(F32)[chunks * MAIN :]
        ends.append([tail[at : at + 2 * EXTRA] for at in range(0, tail.shape[0], 2 * EXTRA)])
    image = lax.broadcasted_iota(jnp.int32, (IMG_DEV, LANES), 0).astype(F32) + 1.0
    half = senders // 2
    first = sum(end[-1] for end in ends[:half])
    second = sum(end[-1] for end in ends[half:])
    both = first + second
    match = jnp.concatenate(
        [image == first[EXTRA : EXTRA + 1], image == second[EXTRA : EXTRA + 1]], axis=1
    ).astype(BF16)
    low = lax.broadcasted_iota(jnp.int32, (IMG_DEV, LANES), 1) % (2 * EXTRA) < EXTRA
    extra = image == both[EXTRA + 1 : EXTRA + 2]
    extras = ((extra & low).astype(BF16), (extra & ~low).astype(BF16))
    total = dot(match, main_ref[...], NN)
    for c in range(chunks):
        tail = jnp.concatenate([end[c // 2] for end in ends], axis=0).astype(BF16)
        out_ref[:, c * LANES : (c + 1) * LANES] = total[:, c * LANES : (c + 1) * LANES] + dot(
            extras[c % 2], tail, NN
        )


def routing_kernel(me_ref, lab_ref, pick_ref, tag_ref):
    me = me_ref[0]
    row = lab_ref[...]
    count = row.shape[1]
    owners = tag_ref.shape[0]
    col = column(row)
    owner_row, owner_col = row // IMG_DEV, col // IMG_DEV
    at = [lax.broadcasted_iota(jnp.int32, (count, count), axis) for axis in range(2)]
    same = owner_col == owner_row
    rank_row = jnp.sum(jnp.where(same & (at[0] < at[1]), 1, 0), axis=0, keepdims=True)
    rank_col = jnp.sum(jnp.where(same & (at[1] < at[0]), 1, 0), axis=1, keepdims=True)
    step = MAIN + 2 * EXTRA
    slot = lax.broadcasted_iota(jnp.int32, (step, count), 0)
    want = jnp.where(slot < MAIN, slot, MAIN + slot % EXTRA)
    hit = want == rank_row
    picks = [jnp.where(hit & (owner_row == owner), F32(1.0), F32(0.0)) for owner in range(owners)]
    pick_ref[...] = jnp.concatenate(picks, axis=0).astype(BF16)
    lane = at[1]
    value = (col % IMG_DEV + 1).astype(F32)
    main_at = (rank_col < MAIN) & (lane - me % (owners // 2) * MAIN == rank_col)
    extra_at = (lane // (2 * EXTRA) == me) & (MAIN + lane % EXTRA == rank_col)
    marks = jnp.concatenate([jnp.where(main_at, value, 0.0), jnp.where(extra_at, value, 0.0)], axis=1)
    mine = lax.broadcasted_iota(jnp.int32, (owners, count), 0) == owner_row
    tags = dot(jnp.where(mine, F32(1.0), F32(0.0)).astype(BF16), marks.astype(BF16), NN)
    sub = lax.broadcasted_iota(jnp.int32, (2 * EXTRA, LANES), 0)
    for owner in range(owners):
        main, extra = tags[owner : owner + 1, :LANES], tags[owner : owner + 1, LANES:]
        tag_ref[owner] = jnp.where(sub == EXTRA, main, jnp.where(sub == EXTRA + 1, extra, 0.0))


def shards(image_raw, text_feat, text_head, image_of_pair, logit_scale, logit_bias):
    rows, width = image_raw.shape[1:]
    owners = lax.axis_size("dp")
    loops = lax.axis_size("loop")
    image, feat, labels = image_raw[0], text_feat[0], image_of_pair[0]
    scalars = (logit_scale[None], logit_bias[None])
    lab = labels[None, :]
    across = [(i, i ^ RING) for i in range(loops)]
    turns = [
        [(i, i & ~(RING - 1) | (i + 1) % RING) for i in range(loops)],
        [(i, i & ~(RING - 1) | (i - 1) % RING) for i in range(loops)],
        [(i, i ^ 2) for i in range(loops)],
    ]

    def ring(value):
        return [lax.ppermute(value, "loop", turn) for turn in turns]

    block = jax.ShapeDtypeStruct((rows, width), BF16)
    wide = jax.ShapeDtypeStruct((rows, width), F32)

    step = MAIN + 2 * EXTRA
    halves = [list(range(at, at + RING)) for at in range(0, loops, RING)]
    picks, tags = call(
        routing_kernel,
        (
            jax.ShapeDtypeStruct((owners * step, rows), BF16),
            jax.ShapeDtypeStruct((owners, 2 * EXTRA, LANES), F32),
        ),
        lax.axis_index("dp")[None], lab, scalars=1,
    )
    far_feat = lax.ppermute(feat, "loop", across)
    x, y, unit_y, inv_y = call(
        embed_kernel, (block, block, wide, jax.ShapeDtypeStruct((rows, 1), F32)), image, feat, text_head
    )
    part = call(near_image_kernel, wide, *scalars, lab, x, y, *ring(y), scalars=2)
    far_x = lax.ppermute(x, "loop", across)
    far_y = call(text_kernel, block, far_feat, text_head)
    far_ys = ring(far_y)
    part, far_x = lax.optimization_barrier((part, far_x))
    sent = call(
        far_image_kernel,
        jax.ShapeDtypeStruct((owners, (MAIN + EXTRA) * width // LANES + EXTRA, LANES), BF16),
        *scalars, image, x, part, far_y, *far_ys, picks, tags, scalars=2,
    )
    sent, x_near = lax.optimization_barrier((sent, x))
    arrived = lax.all_to_all(sent, "dp", split_axis=0, concat_axis=0, tiled=True)
    part_txt = call(near_text_kernel, wide, *scalars, lab, x, y, *ring(x_near), far_x, scalars=2)
    d_text_feat = call(
        text_grad_kernel, wide, *scalars, y, part_txt, *ring(far_x), inv_y, unit_y, text_head,
        scalars=2,
        away=3,
        scratch=[
            pltpu.VMEM((rows, 1), F32),
            pltpu.VMEM((rows, width), F32),
            pltpu.VMEM(text_head.shape, BF16),
            pltpu.SemaphoreType.DMA((3,)),
        ],
    )
    d_image = call(
        sum_kernel,
        jax.ShapeDtypeStruct((IMG_DEV, width), F32),
        arrived,
        scratch=[pltpu.VMEM((owners * MAIN, width), BF16)],
    )
    return (d_text_feat[None], d_image[None])


def solution(mesh):
    placed = (P("dp", "loop", None), P("dp", "loop", None), P(), P("dp", "loop"), P(), P())
    return jax.shard_map(
        shards,
        mesh=mesh,
        in_specs=placed,
        out_specs=(P("dp", "loop", None), P("loop", "dp", None)),
        check_vma=False,
    )
```

```python
import jax
import jax.numpy as jnp
from jax import lax
from jax.experimental import pallas as pl
from jax.experimental.pallas import tpu as pltpu
from jax.sharding import PartitionSpec as P

EPS = 1e-06
IMG_DEV = 64
RING = 4
LANES = 128
MAIN = 16
EXTRA = 4
NEAR_COST = 28_825_000_000
TAIL_COST = 23_060_000_000
F32 = jnp.float32
BF16 = jnp.bfloat16

NT = ((1,), (1,))
NN = ((1,), (0,))
TN = ((0,), (0,))


def call(kernel, outs, *operands, scalars=0, away=0, scratch=(), flops=0):
    smem = pl.BlockSpec(memory_space=pltpu.SMEM)
    vmem = pl.BlockSpec(memory_space=pltpu.VMEM)
    return pl.pallas_call(
        kernel,
        out_shape=outs,
        in_specs=[smem] * scalars
        + [vmem] * (len(operands) - scalars - away)
        + [pl.BlockSpec(memory_space=pl.ANY)] * away,
        scratch_shapes=scratch,
        compiler_params=pltpu.CompilerParams(vmem_limit_bytes=48 * 2**20),
        cost_estimate=pl.CostEstimate(flops=flops, bytes_accessed=flops // 300, transcendentals=0) if flops else None,
    )(*operands)


def inv_norm(values):
    return lax.rsqrt(jnp.sum(values * values, axis=-1, keepdims=True) + EPS)


def dot(a, b, dims):
    return lax.dot_general(a, b, (dims, ((), ())), preferred_element_type=F32)


def embed_kernel(img_ref, feat_ref, head_ref, x_ref, y_ref, unit_ref, inv_ref):
    x = img_ref[...].astype(F32)
    x_ref[...] = (x * inv_norm(x)).astype(BF16)
    pre = dot(feat_ref[...], head_ref[...], NN)
    inv = inv_norm(pre)
    unit = pre * inv
    y_ref[...] = unit.astype(BF16)
    unit_ref[...] = unit
    inv_ref[...] = inv


def text_kernel(feat_ref, head_ref, emb_ref):
    pre = dot(feat_ref[...], head_ref[...], NN)
    emb_ref[...] = (pre * inv_norm(pre)).astype(BF16)


def apart_weights(own, others, scale, shift):
    logits = scale * dot(own, others, NT) + shift
    return (1.0 / (1.0 + jnp.exp(-logits))).astype(BF16)


def column(row):
    size = row.shape[1]
    at = [lax.broadcasted_iota(jnp.int32, (size, size), axis) for axis in range(2)]
    return jnp.sum(jnp.where(at[0] == at[1], row, 0), axis=1, keepdims=True)


def home_weights(x, y, lab_ref, scale, shift):
    lab = lab_ref[...]
    sign = jnp.where(column(lab) == lab, F32(1.0), F32(-1.0))
    logits = scale * dot(x, y, NT) + shift
    return (-sign / (1.0 + jnp.exp(sign * logits))).astype(BF16)


def near_image_kernel(scale_ref, shift_ref, lab_ref, x_ref, y_ref, a_ref, b_ref, c_ref, out_ref):
    scale, shift = scale_ref[0], shift_ref[0]
    x, y = x_ref[...], y_ref[...]
    home = home_weights(x, y, lab_ref, scale, shift)
    others = jnp.concatenate([a_ref[...], b_ref[...], c_ref[...]], axis=0)
    out_ref[...] = dot(home, y, NN) + dot(apart_weights(x, others, scale, shift), others, NN)


def far_image_kernel(
    scale_ref, shift_ref, raw_ref, x_ref, part_ref, a_ref, b_ref, c_ref, d_ref, pick_ref, tag_ref, out_ref
):
    scale, shift = scale_ref[0], shift_ref[0]
    others = jnp.concatenate([a_ref[...], b_ref[...], c_ref[...], d_ref[...]], axis=0)
    weight = apart_weights(x_ref[...], others, scale, shift)
    grad = scale * (part_ref[...] + dot(weight, others, NN))
    x = raw_ref[...].astype(F32)
    inv = inv_norm(x)
    unit = x * inv
    pair = (grad - unit * jnp.sum(unit * grad, axis=-1, keepdims=True)) * inv
    sent = dot(pick_ref[...], pair.astype(BF16), NN)
    low = lax.broadcasted_iota(jnp.int32, (2 * EXTRA, LANES), 0) < EXTRA
    step = MAIN + 2 * EXTRA
    for owner in range(out_ref.shape[0]):
        rows = sent[owner * step : (owner + 1) * step]
        cols = [rows[:, at : at + LANES] for at in range(0, rows.shape[1], LANES)]
        ends = [col[MAIN:] for col in cols] + [tag_ref[owner]]
        pairs = [jnp.where(low, ends[at], ends[at + 1]) for at in range(0, len(ends), 2)]
        out_ref[owner] = jnp.concatenate([col[:MAIN] for col in cols] + pairs, axis=0).astype(BF16)


def near_text_kernel(scale_ref, shift_ref, lab_ref, x_ref, y_ref, a_ref, b_ref, c_ref, d_ref, out_ref):
    scale, shift = scale_ref[0], shift_ref[0]
    x, y = x_ref[...], y_ref[...]
    home = home_weights(x, y, lab_ref, scale, shift)
    others = jnp.concatenate([a_ref[...], b_ref[...], c_ref[...], d_ref[...]], axis=0)
    out_ref[...] = dot(home, x, TN) + dot(apart_weights(y, others, scale, shift), others, NN)


def text_grad_kernel(
    scale_ref, shift_ref, y_ref, part_ref, a_ref, b_ref, c_ref, inv_hbm, unit_hbm, head_hbm, out_ref,
    inv_ref, unit_ref, head_ref, sems,
):
    scale, shift = scale_ref[0], shift_ref[0]
    pairs = ((inv_hbm, inv_ref), (unit_hbm, unit_ref), (head_hbm, head_ref))
    copies = [pltpu.make_async_copy(src, dst, sems.at[at]) for at, (src, dst) in enumerate(pairs)]
    for copy in copies:
        copy.start()
    others = jnp.concatenate([a_ref[...], b_ref[...], c_ref[...]], axis=0)
    weight = apart_weights(y_ref[...], others, scale, shift)
    grad = scale * (part_ref[...] + dot(weight, others, NN))
    copies[0].wait()
    copies[1].wait()
    unit = unit_ref[...]
    pre = (grad - unit * jnp.sum(unit * grad, axis=-1, keepdims=True)) * inv_ref[...]
    copies[2].wait()
    out_ref[...] = dot(pre.astype(BF16), head_ref[...], NT)


def sum_kernel(arrived_ref, out_ref, main_ref):
    senders = arrived_ref.shape[0]
    chunks = out_ref.shape[1] // LANES
    ends = []
    for sender in range(senders):
        block = arrived_ref[sender]
        for c in range(chunks):
            main_ref[sender * MAIN : (sender + 1) * MAIN, c * LANES : (c + 1) * LANES] = block[
                c * MAIN : (c + 1) * MAIN
            ]
        tail = block.astype(F32)[chunks * MAIN :]
        ends.append([tail[at : at + 2 * EXTRA] for at in range(0, tail.shape[0], 2 * EXTRA)])
    image = lax.broadcasted_iota(jnp.int32, (IMG_DEV, LANES), 0).astype(F32) + 1.0
    half = senders // 2
    first = sum(end[-1] for end in ends[:half])
    second = sum(end[-1] for end in ends[half:])
    both = first + second
    match = jnp.concatenate(
        [image == first[EXTRA : EXTRA + 1], image == second[EXTRA : EXTRA + 1]], axis=1
    ).astype(BF16)
    low = lax.broadcasted_iota(jnp.int32, (IMG_DEV, LANES), 1) % (2 * EXTRA) < EXTRA
    extra = image == both[EXTRA + 1 : EXTRA + 2]
    extras = ((extra & low).astype(BF16), (extra & ~low).astype(BF16))
    total = dot(match, main_ref[...], NN)
    for c in range(chunks):
        tail = jnp.concatenate([end[c // 2] for end in ends], axis=0).astype(BF16)
        out_ref[:, c * LANES : (c + 1) * LANES] = total[:, c * LANES : (c + 1) * LANES] + dot(
            extras[c % 2], tail, NN
        )


def routing_kernel(me_ref, lab_ref, pick_ref, tag_ref):
    me = me_ref[0]
    row = lab_ref[...]
    count = row.shape[1]
    owners = tag_ref.shape[0]
    col = column(row)
    owner_row, owner_col = row // IMG_DEV, col // IMG_DEV
    at = [lax.broadcasted_iota(jnp.int32, (count, count), axis) for axis in range(2)]
    same = owner_col == owner_row
    rank_row = jnp.sum(jnp.where(same & (at[0] < at[1]), 1, 0), axis=0, keepdims=True)
    rank_col = jnp.sum(jnp.where(same & (at[1] < at[0]), 1, 0), axis=1, keepdims=True)
    step = MAIN + 2 * EXTRA
    slot = lax.broadcasted_iota(jnp.int32, (step, count), 0)
    want = jnp.where(slot < MAIN, slot, MAIN + slot % EXTRA)
    hit = want == rank_row
    picks = [jnp.where(hit & (owner_row == owner), F32(1.0), F32(0.0)) for owner in range(owners)]
    pick_ref[...] = jnp.concatenate(picks, axis=0).astype(BF16)
    lane = at[1]
    value = (col % IMG_DEV + 1).astype(F32)
    main_at = (rank_col < MAIN) & (lane - me % (owners // 2) * MAIN == rank_col)
    extra_at = (lane // (2 * EXTRA) == me) & (MAIN + lane % EXTRA == rank_col)
    marks = jnp.concatenate([jnp.where(main_at, value, 0.0), jnp.where(extra_at, value, 0.0)], axis=1)
    mine = lax.broadcasted_iota(jnp.int32, (owners, count), 0) == owner_row
    tags = dot(jnp.where(mine, F32(1.0), F32(0.0)).astype(BF16), marks.astype(BF16), NN)
    sub = lax.broadcasted_iota(jnp.int32, (2 * EXTRA, LANES), 0)
    for owner in range(owners):
        main, extra = tags[owner : owner + 1, :LANES], tags[owner : owner + 1, LANES:]
        tag_ref[owner] = jnp.where(sub == EXTRA, main, jnp.where(sub == EXTRA + 1, extra, 0.0))


def shards(image_raw, text_feat, text_head, image_of_pair, logit_scale, logit_bias):
    rows, width = image_raw.shape[1:]
    owners = lax.axis_size("dp")
    loops = lax.axis_size("loop")
    image, feat, labels = image_raw[0], text_feat[0], image_of_pair[0]
    scalars = (logit_scale[None], logit_bias[None])
    lab = labels[None, :]
    across = [(i, i ^ RING) for i in range(loops)]
    turns = [
        [(i, i & ~(RING - 1) | (i + 1) % RING) for i in range(loops)],
        [(i, i & ~(RING - 1) | (i - 1) % RING) for i in range(loops)],
        [(i, i ^ 2) for i in range(loops)],
    ]

    def ring(value):
        return [lax.ppermute(value, "loop", turn) for turn in turns]

    block = jax.ShapeDtypeStruct((rows, width), BF16)
    wide = jax.ShapeDtypeStruct((rows, width), F32)

    step = MAIN + 2 * EXTRA
    halves = [list(range(at, at + RING)) for at in range(0, loops, RING)]
    picks, tags = call(
        routing_kernel,
        (
            jax.ShapeDtypeStruct((owners * step, rows), BF16),
            jax.ShapeDtypeStruct((owners, 2 * EXTRA, LANES), F32),
        ),
        lax.axis_index("dp")[None], lab, scalars=1,
    )
    far_feat = lax.ppermute(feat, "loop", across)
    x, y, unit_y, inv_y = call(
        embed_kernel, (block, block, wide, jax.ShapeDtypeStruct((rows, 1), F32)), image, feat, text_head
    )
    part = call(near_image_kernel, wide, *scalars, lab, x, y, *ring(y), scalars=2, flops=NEAR_COST)
    far_x = lax.ppermute(x, "loop", across)
    far_y = call(text_kernel, block, far_feat, text_head)
    far_ys = ring(far_y)
    sent = call(
        far_image_kernel,
        jax.ShapeDtypeStruct((owners, (MAIN + EXTRA) * width // LANES + EXTRA, LANES), BF16),
        *scalars, image, x, part, far_y, *far_ys, picks, tags, scalars=2,
    )
    sent, x_near = lax.optimization_barrier((sent, x))
    x_near, far_x = lax.optimization_barrier((x_near, far_x))
    arrived = lax.all_to_all(sent, "dp", split_axis=0, concat_axis=0, tiled=True)
    part_txt = call(near_text_kernel, wide, *scalars, lab, x, y, *ring(x_near), far_x, scalars=2)
    d_text_feat = call(
        text_grad_kernel, wide, *scalars, y, part_txt, *ring(far_x), inv_y, unit_y, text_head,
        scalars=2,
        away=3,
        flops=TAIL_COST,
        scratch=[
            pltpu.VMEM((rows, 1), F32),
            pltpu.VMEM((rows, width), F32),
            pltpu.VMEM(text_head.shape, BF16),
            pltpu.SemaphoreType.DMA((3,)),
        ],
    )
    d_image = call(
        sum_kernel,
        jax.ShapeDtypeStruct((IMG_DEV, width), F32),
        arrived,
        scratch=[pltpu.VMEM((owners * MAIN, width), BF16)],
    )
    return (d_text_feat[None], d_image[None])


def solution(mesh):
    placed = (P("dp", "loop", None), P("dp", "loop", None), P(), P("dp", "loop"), P(), P())
    return jax.shard_map(
        shards,
        mesh=mesh,
        in_specs=placed,
        out_specs=(P("dp", "loop", None), P("loop", "dp", None)),
        check_vma=False,
    )
```

```python
import jax
import jax.numpy as jnp
from jax import lax
from jax.experimental import pallas as pl
from jax.experimental.pallas import tpu as pltpu
from jax.sharding import PartitionSpec as P

EPS = 1e-06
IMG_DEV = 64
RING = 4
LANES = 128
MAIN = 16
EXTRA = 4
NEAR_COST = 28_825_000_000
TAIL_COST = 23_060_000_000
F32 = jnp.float32
BF16 = jnp.bfloat16

NT = ((1,), (1,))
NN = ((1,), (0,))
TN = ((0,), (0,))


def call(kernel, outs, *operands, scalars=0, away=0, ahead=0, scratch=(), flops=0):
    smem = pl.BlockSpec(memory_space=pltpu.SMEM)
    vmem = pl.BlockSpec(memory_space=pltpu.VMEM)
    return pl.pallas_call(
        kernel,
        out_shape=outs,
        in_specs=[smem] * scalars
        + [pl.BlockSpec(memory_space=pl.ANY)] * ahead
        + [vmem] * (len(operands) - scalars - away - ahead)
        + [pl.BlockSpec(memory_space=pl.ANY)] * away,
        scratch_shapes=scratch,
        compiler_params=pltpu.CompilerParams(vmem_limit_bytes=48 * 2**20),
        cost_estimate=pl.CostEstimate(flops=flops, bytes_accessed=flops // 300, transcendentals=0) if flops else None,
    )(*operands)


def inv_norm(values):
    return lax.rsqrt(jnp.sum(values * values, axis=-1, keepdims=True) + EPS)


def dot(a, b, dims):
    return lax.dot_general(a, b, (dims, ((), ())), preferred_element_type=F32)


def embed_kernel(img_ref, feat_ref, head_ref, x_ref, y_ref, unit_ref, inv_ref):
    x = img_ref[...].astype(F32)
    x_ref[...] = (x * inv_norm(x)).astype(BF16)
    pre = dot(feat_ref[...], head_ref[...], NN)
    inv = inv_norm(pre)
    unit = pre * inv
    y_ref[...] = unit.astype(BF16)
    unit_ref[...] = unit
    inv_ref[...] = inv


def text_kernel(feat_ref, head_ref, emb_ref):
    pre = dot(feat_ref[...], head_ref[...], NN)
    emb_ref[...] = (pre * inv_norm(pre)).astype(BF16)


def apart_weights(own, others, scale, shift):
    logits = scale * dot(own, others, NT) + shift
    return (1.0 / (1.0 + jnp.exp(-logits))).astype(BF16)


def column(row):
    size = row.shape[1]
    at = [lax.broadcasted_iota(jnp.int32, (size, size), axis) for axis in range(2)]
    return jnp.sum(jnp.where(at[0] == at[1], row, 0), axis=1, keepdims=True)


def home_weights(x, y, lab_ref, scale, shift):
    lab = lab_ref[...]
    sign = jnp.where(column(lab) == lab, F32(1.0), F32(-1.0))
    logits = scale * dot(x, y, NT) + shift
    return (-sign / (1.0 + jnp.exp(sign * logits))).astype(BF16)


def near_image_kernel(scale_ref, shift_ref, lab_ref, x_ref, y_ref, a_ref, b_ref, c_ref, out_ref):
    scale, shift = scale_ref[0], shift_ref[0]
    x, y = x_ref[...], y_ref[...]
    home = home_weights(x, y, lab_ref, scale, shift)
    others = jnp.concatenate([a_ref[...], b_ref[...], c_ref[...]], axis=0)
    out_ref[...] = dot(home, y, NN) + dot(apart_weights(x, others, scale, shift), others, NN)


def far_image_kernel(
    scale_ref, shift_ref, raw_ref, x_ref, part_ref, a_ref, b_ref, c_ref, d_ref, pick_ref, tag_ref, out_ref
):
    scale, shift = scale_ref[0], shift_ref[0]
    others = jnp.concatenate([a_ref[...], b_ref[...], c_ref[...], d_ref[...]], axis=0)
    weight = apart_weights(x_ref[...], others, scale, shift)
    grad = scale * (part_ref[...] + dot(weight, others, NN))
    x = raw_ref[...].astype(F32)
    inv = inv_norm(x)
    unit = x * inv
    pair = (grad - unit * jnp.sum(unit * grad, axis=-1, keepdims=True)) * inv
    sent = dot(pick_ref[...], pair.astype(BF16), NN)
    low = lax.broadcasted_iota(jnp.int32, (2 * EXTRA, LANES), 0) < EXTRA
    step = MAIN + 2 * EXTRA
    for owner in range(out_ref.shape[0]):
        rows = sent[owner * step : (owner + 1) * step]
        cols = [rows[:, at : at + LANES] for at in range(0, rows.shape[1], LANES)]
        ends = [col[MAIN:] for col in cols] + [tag_ref[owner]]
        pairs = [jnp.where(low, ends[at], ends[at + 1]) for at in range(0, len(ends), 2)]
        out_ref[owner] = jnp.concatenate([col[:MAIN] for col in cols] + pairs, axis=0).astype(BF16)


def near_text_kernel(scale_ref, shift_ref, lab_ref, x_ref, y_ref, a_ref, b_ref, c_ref, d_ref, out_ref):
    scale, shift = scale_ref[0], shift_ref[0]
    x, y = x_ref[...], y_ref[...]
    home = home_weights(x, y, lab_ref, scale, shift)
    others = jnp.concatenate([a_ref[...], b_ref[...], c_ref[...], d_ref[...]], axis=0)
    out_ref[...] = dot(home, x, TN) + dot(apart_weights(y, others, scale, shift), others, NN)


def text_grad_kernel(
    scale_ref, shift_ref, part_hbm, y_ref, a_ref, b_ref, c_ref, inv_hbm, unit_hbm, head_hbm, out_ref,
    part_ref, inv_ref, unit_ref, head_ref, sems,
):
    scale, shift = scale_ref[0], shift_ref[0]
    pairs = ((part_hbm, part_ref), (inv_hbm, inv_ref), (unit_hbm, unit_ref), (head_hbm, head_ref))
    copies = [pltpu.make_async_copy(src, dst, sems.at[at]) for at, (src, dst) in enumerate(pairs)]
    for copy in copies:
        copy.start()
    others = jnp.concatenate([a_ref[...], b_ref[...], c_ref[...]], axis=0)
    weight = apart_weights(y_ref[...], others, scale, shift)
    far = dot(weight, others, NN)
    for copy in copies[:3]:
        copy.wait()
    grad = scale * (part_ref[...] + far)
    unit = unit_ref[...]
    pre = (grad - unit * jnp.sum(unit * grad, axis=-1, keepdims=True)) * inv_ref[...]
    copies[3].wait()
    out_ref[...] = dot(pre.astype(BF16), head_ref[...], NT)


def sum_kernel(arrived_ref, out_ref, main_ref):
    senders = arrived_ref.shape[0]
    chunks = out_ref.shape[1] // LANES
    ends = []
    for sender in range(senders):
        block = arrived_ref[sender]
        for c in range(chunks):
            main_ref[sender * MAIN : (sender + 1) * MAIN, c * LANES : (c + 1) * LANES] = block[
                c * MAIN : (c + 1) * MAIN
            ]
        tail = block.astype(F32)[chunks * MAIN :]
        ends.append([tail[at : at + 2 * EXTRA] for at in range(0, tail.shape[0], 2 * EXTRA)])
    image = lax.broadcasted_iota(jnp.int32, (IMG_DEV, LANES), 0).astype(F32) + 1.0
    half = senders // 2
    first = sum(end[-1] for end in ends[:half])
    second = sum(end[-1] for end in ends[half:])
    both = first + second
    match = jnp.concatenate(
        [image == first[EXTRA : EXTRA + 1], image == second[EXTRA : EXTRA + 1]], axis=1
    ).astype(BF16)
    low = lax.broadcasted_iota(jnp.int32, (IMG_DEV, LANES), 1) % (2 * EXTRA) < EXTRA
    extra = image == both[EXTRA + 1 : EXTRA + 2]
    extras = ((extra & low).astype(BF16), (extra & ~low).astype(BF16))
    total = dot(match, main_ref[...], NN)
    for c in range(chunks):
        tail = jnp.concatenate([end[c // 2] for end in ends], axis=0).astype(BF16)
        out_ref[:, c * LANES : (c + 1) * LANES] = total[:, c * LANES : (c + 1) * LANES] + dot(
            extras[c % 2], tail, NN
        )


def routing_kernel(me_ref, lab_ref, pick_ref, tag_ref):
    me = me_ref[0]
    row = lab_ref[...]
    count = row.shape[1]
    owners = tag_ref.shape[0]
    col = column(row)
    owner_row, owner_col = row // IMG_DEV, col // IMG_DEV
    at = [lax.broadcasted_iota(jnp.int32, (count, count), axis) for axis in range(2)]
    same = owner_col == owner_row
    rank_row = jnp.sum(jnp.where(same & (at[0] < at[1]), 1, 0), axis=0, keepdims=True)
    rank_col = jnp.sum(jnp.where(same & (at[1] < at[0]), 1, 0), axis=1, keepdims=True)
    step = MAIN + 2 * EXTRA
    slot = lax.broadcasted_iota(jnp.int32, (step, count), 0)
    want = jnp.where(slot < MAIN, slot, MAIN + slot % EXTRA)
    hit = want == rank_row
    picks = [jnp.where(hit & (owner_row == owner), F32(1.0), F32(0.0)) for owner in range(owners)]
    pick_ref[...] = jnp.concatenate(picks, axis=0).astype(BF16)
    lane = at[1]
    value = (col % IMG_DEV + 1).astype(F32)
    main_at = (rank_col < MAIN) & (lane - me % (owners // 2) * MAIN == rank_col)
    extra_at = (lane // (2 * EXTRA) == me) & (MAIN + lane % EXTRA == rank_col)
    marks = jnp.concatenate([jnp.where(main_at, value, 0.0), jnp.where(extra_at, value, 0.0)], axis=1)
    mine = lax.broadcasted_iota(jnp.int32, (owners, count), 0) == owner_row
    tags = dot(jnp.where(mine, F32(1.0), F32(0.0)).astype(BF16), marks.astype(BF16), NN)
    sub = lax.broadcasted_iota(jnp.int32, (2 * EXTRA, LANES), 0)
    for owner in range(owners):
        main, extra = tags[owner : owner + 1, :LANES], tags[owner : owner + 1, LANES:]
        tag_ref[owner] = jnp.where(sub == EXTRA, main, jnp.where(sub == EXTRA + 1, extra, 0.0))


def shards(image_raw, text_feat, text_head, image_of_pair, logit_scale, logit_bias):
    rows, width = image_raw.shape[1:]
    owners = lax.axis_size("dp")
    loops = lax.axis_size("loop")
    image, feat, labels = image_raw[0], text_feat[0], image_of_pair[0]
    scalars = (logit_scale[None], logit_bias[None])
    lab = labels[None, :]
    across = [(i, i ^ RING) for i in range(loops)]
    turns = [
        [(i, i & ~(RING - 1) | (i + 1) % RING) for i in range(loops)],
        [(i, i & ~(RING - 1) | (i - 1) % RING) for i in range(loops)],
        [(i, i ^ 2) for i in range(loops)],
    ]

    def ring(value):
        return [lax.ppermute(value, "loop", turn) for turn in turns]

    block = jax.ShapeDtypeStruct((rows, width), BF16)
    wide = jax.ShapeDtypeStruct((rows, width), F32)

    step = MAIN + 2 * EXTRA
    halves = [list(range(at, at + RING)) for at in range(0, loops, RING)]
    picks, tags = call(
        routing_kernel,
        (
            jax.ShapeDtypeStruct((owners * step, rows), BF16),
            jax.ShapeDtypeStruct((owners, 2 * EXTRA, LANES), F32),
        ),
        lax.axis_index("dp")[None], lab, scalars=1,
    )
    far_feat = lax.ppermute(feat, "loop", across)
    x, y, unit_y, inv_y = call(
        embed_kernel, (block, block, wide, jax.ShapeDtypeStruct((rows, 1), F32)), image, feat, text_head
    )
    part = call(near_image_kernel, wide, *scalars, lab, x, y, *ring(y), scalars=2, flops=NEAR_COST)
    far_x = lax.ppermute(x, "loop", across)
    far_y = call(text_kernel, block, far_feat, text_head)
    far_ys = ring(far_y)
    sent = call(
        far_image_kernel,
        jax.ShapeDtypeStruct((owners, (MAIN + EXTRA) * width // LANES + EXTRA, LANES), BF16),
        *scalars, image, x, part, far_y, *far_ys, picks, tags, scalars=2,
    )
    sent, x_near = lax.optimization_barrier((sent, x))
    x_near, far_x = lax.optimization_barrier((x_near, far_x))
    arrived = lax.all_to_all(sent, "dp", split_axis=0, concat_axis=0, tiled=True)
    part_txt = call(near_text_kernel, wide, *scalars, lab, x, y, *ring(x_near), far_x, scalars=2)
    d_text_feat = call(
        text_grad_kernel, wide, *scalars, part_txt, y, *ring(far_x), inv_y, unit_y, text_head,
        scalars=2,
        away=3,
        ahead=1,
        flops=TAIL_COST,
        scratch=[
            pltpu.VMEM((rows, width), F32),
            pltpu.VMEM((rows, 1), F32),
            pltpu.VMEM((rows, width), F32),
            pltpu.VMEM(text_head.shape, BF16),
            pltpu.SemaphoreType.DMA((4,)),
        ],
    )
    d_image = call(
        sum_kernel,
        jax.ShapeDtypeStruct((IMG_DEV, width), F32),
        arrived,
        scratch=[pltpu.VMEM((owners * MAIN, width), BF16)],
    )
    return (d_text_feat[None], d_image[None])


def solution(mesh):
    placed = (P("dp", "loop", None), P("dp", "loop", None), P(), P("dp", "loop"), P(), P())
    return jax.shard_map(
        shards,
        mesh=mesh,
        in_specs=placed,
        out_specs=(P("dp", "loop", None), P("loop", "dp", None)),
        check_vma=False,
    )
```
